512 devices in a mesh: band: 8 (over x, z_hi), space: 64 (over z_lo, y, core).
Axes of the slice: x: 4, y: 8, z: 8 (z_hi: 2, z_lo: 4; z = z_hi * 4 + z_lo), core: 2. Of those that a mesh axis runs over, the one named last changes fastest.
Arguments:
- prior_orbitals: float32 [384, 64, 8, 8, 128], P('band', 'space'), may hold values from -6 to 6
- orbital_block: float32 [128, 64, 8, 8, 128], P('band', 'space'), may hold values from -6 to 6
- potential: float32 [64, 8, 8, 128], P('space'), may hold values from -2 to 1
- prior_rotation: float32 [384, 128], P('band'), may hold values from -0.25 to 0.25
- block_rotation: float32 [128, 128], replicated, may hold values from -0.25 to 0.25
Outputs:
- filtered: float32 [128, 64, 8, 8, 128], P('band', 'space')
- ritz_columns: float32 [128, 64, 8, 8, 128], P('band', 'space')
The draws below stay inside these ranges and needn't reach their ends.
All inputs are finite; a program needn't handle non-finite values.
Results may differ from the reference program's by a relative error of at most 0.00007.
Values sent between devices are 32-bit elements; how exact they have to be, the bound alone decides.
A program may use at most 64 MiB of HBM per device.

```python
import jax
import jax.numpy as jnp
from jax import lax

NBLK = 128
NPREV = 384
NRITZ = 128
CX = 8
CY = 8
CZ = 128
NDOM = 64
NX = 8
NY = 512
NZ = 128


def shard_levels(rng, extent, shards, least, high):
    loudness, own = 1.0, jax.random.fold_in(rng, 6)
    for axis_at, shards_of in shards:
        steps = jnp.exp(jax.random.uniform(jax.random.fold_in(own, axis_at), (shards_of,), jnp.float32, least / len(shards), high / len(shards)))
        loudness = loudness * jnp.repeat(steps, extent[axis_at] // shards_of).reshape([-1 if axis == axis_at else 1 for axis in range(len(extent))])
    return loudness


def noise(own_key, dims, width, bound, shards=(), dtype=jnp.bfloat16):
    values = jax.random.normal(own_key, dims, jnp.float32) * width
    if len(shards) > 0:
        values = shard_levels(own_key, dims, shards, -0.22, 0.18) * values
    return jnp.clip(values, min=-bound, max=bound).astype(dtype)


def setup_inputs(seed: int = 0) -> dict:
    arg_keys = jax.random.split(jax.random.key(seed), 6)
    return {
        "prior_orbitals": noise(arg_keys[0], (NPREV, NDOM, CX, CY, CZ), 1.0, 6.0, ((0, 8), (1, 64)), jnp.float32),
        "orbital_block": noise(arg_keys[1], (NBLK, NDOM, CX, CY, CZ), 1.0, 6.0, ((0, 8), (1, 64)), jnp.float32),
        "potential": jnp.clip(-2.0 + 3.0 * jax.random.uniform(arg_keys[2], (NDOM, CX, CY, CZ), jnp.float32) ** shard_levels(arg_keys[2], (NDOM, CX, CY, CZ), ((0, 64),), -0.2, 0.2), -2.0, 1.0),
        "prior_rotation": noise(arg_keys[3], (NPREV, NRITZ), (NPREV + NBLK) ** -0.5, 0.25, ((0, 8),), jnp.float32),
        "block_rotation": noise(arg_keys[4], (NBLK, NRITZ), (NPREV + NBLK) ** -0.5, 0.25, (), jnp.float32),
    }


stencil_taps = (-5369.0 / 1800.0, 12.0 / 7.0, -15.0 / 56.0, 10.0 / 189.0, -1.0 / 112.0, 2.0 / 1925.0, -1.0 / 16632.0)
stencil_reach = 6
shift_center = 6.0
half_range = 5.0


def to_grid(blocks):
    orbitals = blocks.shape[0]
    return blocks.transpose(0, 2, 1, 3, 4).reshape(orbitals, NX, NY, NZ)


def to_blocks(grid_values):
    orbitals = grid_values.shape[0]
    shaped = grid_values.reshape(orbitals, CX, NDOM, CY, CZ)
    return shaped.transpose(0, 2, 1, 3, 4)


def second_along(padded, axis_number, length):
    summed = stencil_taps[0] * lax.slice_in_dim(padded, stencil_reach, stencil_reach + length, axis=axis_number)
    for offset in range(1, stencil_reach + 1):
        ahead = lax.slice_in_dim(padded, stencil_reach + offset, stencil_reach + offset + length, axis=axis_number)
        behind = lax.slice_in_dim(padded, stencil_reach - offset, stencil_reach - offset + length, axis=axis_number)
        summed = summed + stencil_taps[offset] * (ahead + behind)
    return summed


def hamiltonian(values_in, potential_grid):
    pad_x = jnp.pad(values_in, ((0, 0), (stencil_reach, stencil_reach), (0, 0), (0, 0)))
    pad_y = jnp.pad(values_in, ((0, 0), (0, 0), (stencil_reach, stencil_reach), (0, 0)))
    pad_z = jnp.pad(values_in, ((0, 0), (0, 0), (0, 0), (stencil_reach, stencil_reach)))
    laplace = second_along(pad_x, 1, NX) + second_along(pad_y, 2, NY) + second_along(pad_z, 3, NZ)
    return -0.5 * laplace + potential_grid * values_in


def reference(prior_orbitals, orbital_block, potential, prior_rotation, block_rotation):
    potential_grid = to_grid(potential[None])[0]
    start_grid = to_grid(orbital_block)
    first_step = (hamiltonian(start_grid, potential_grid) - shift_center * start_grid) / half_range
    second_step = 2.0 * (hamiltonian(first_step, potential_grid) - shift_center * first_step) / half_range - start_grid
    filtered = to_blocks(second_step)
    cell_count = NDOM * CX * CY * CZ
    ritz_flat = jnp.dot(prior_rotation.T, prior_orbitals.reshape(NPREV, cell_count), precision=lax.Precision.HIGHEST, preferred_element_type=jnp.float32)
    ritz_flat = ritz_flat + jnp.dot(block_rotation.T, filtered.reshape(NBLK, cell_count), precision=lax.Precision.HIGHEST, preferred_element_type=jnp.float32)
    return filtered, ritz_flat.reshape(NRITZ, NDOM, CX, CY, CZ)
```

```python
import functools

import jax
import jax.numpy as jnp
from jax import lax
from jax.experimental import pallas as pl
from jax.experimental.pallas import tpu as pltpu
from jax.sharding import PartitionSpec as P

stencil_taps = (
    -5369.0 / 1800.0,
    12.0 / 7.0,
    -15.0 / 56.0,
    10.0 / 189.0,
    -1.0 / 112.0,
    2.0 / 1925.0,
    -1.0 / 16632.0,
)
reach = 6
shift_center = 6.0
half_range = 5.0
lap_scale = -0.5 / half_range

NB = 16
NP = 48
CX = 8
CY = 8
CZ = 128
XS = 4
ZH = 2
NCOL = 128
CHUNKS = 4
PER = NB // CHUNKS
MESH = pl.DeviceIdType.MESH
f32 = jnp.float32
bf16 = jnp.bfloat16


def split(values):
    high = values.astype(bf16)
    low = (values - high.astype(f32)).astype(bf16)
    return high, low


def dot(lhs, rhs):
    return jnp.dot(lhs, rhs, preferred_element_type=f32)


def stencil(ext, at, band, diagonal):
    cells = ext[at, :, 8:16, :]
    high, low = split(cells.reshape(CX * CY, CZ))
    along_z = dot(jnp.concatenate([high, low, high], axis=1), band[...]).reshape(CX, CY, CZ)
    planes = [cells[i] for i in range(CX)]
    rows = []
    for i in range(CX):
        total = along_z[i] + diagonal[i] * planes[i]
        for k in range(1, reach + 1):
            near = ext[at, i, 8 - k : 16 - k, :] + ext[at, i, 8 + k : 16 + k, :]
            if i - k >= 0:
                near = near + planes[i - k]
            if i + k < CX:
                near = near + planes[i + k]
            total = total + (lap_scale * stencil_taps[k]) * near
        rows.append(total)
    return rows


def kernel(
    slabs,
    prior,
    block,
    pot,
    prior_rot,
    block_rot,
    filtered_out,
    ritz_out,
    ext0,
    ext1,
    fil,
    gp,
    gf,
    wp,
    wp_high,
    wp_low,
    wf,
    band,
    diagonal,
    pp,
    zr,
    sm,
    local_sem,
    halo_send,
    halo_recv,
    wp_send,
    wp_recv,
    gp_send,
    gp_recv,
    gf_send,
    gf_recv,
    z_send,
    z_recv,
    out_send,
    out_recv,
):
    b = lax.axis_index("band")
    d = lax.axis_index("space")
    x = lax.div(b, ZH)
    zh = lax.rem(b, ZH)
    has_prev = d > 0
    has_next = d < slabs - 1

    def x_of(r):
        return lax.rem(x + r, XS)

    def x_peer(r):
        return (x_of(r) * ZH + zh, d)

    z_peer = (x * ZH + (1 - zh), d)
    prev_peer = (b, jnp.maximum(d - 1, 0))
    next_peer = (b, jnp.minimum(d + 1, slabs - 1))

    barrier = pltpu.get_barrier_semaphore()
    for r in range(1, XS):
        pl.semaphore_signal(barrier, inc=1, device_id=x_peer(r), device_id_type=MESH)
    pl.semaphore_signal(barrier, inc=1, device_id=z_peer, device_id_type=MESH)

    @pl.when(has_prev)
    def _():
        pl.semaphore_signal(barrier, inc=1, device_id=prev_peer, device_id_type=MESH)

    @pl.when(has_next)
    def _():
        pl.semaphore_signal(barrier, inc=1, device_id=next_peer, device_id_type=MESH)

    def remote(src, dst, send, recv, peer):
        return pltpu.make_async_remote_copy(
            src_ref=src, dst_ref=dst, send_sem=send, recv_sem=recv, device_id=peer, device_id_type=MESH
        )

    def chunk(c):
        return pl.ds(c * PER, PER)

    own_block = [
        pltpu.make_async_copy(block.at[chunk(c), 0], ext0.at[chunk(c), :, pl.ds(8, 8), :], local_sem.at[c])
        for c in range(CHUNKS)
    ]
    own_prior = [
        pltpu.make_async_copy(prior.at[:, 0, 2 * x + xp], gp.at[xp, x], local_sem.at[CHUNKS + xp])
        for xp in range(2)
    ]
    own_fil = [
        pltpu.make_async_copy(
            fil.at[chunk(c), pl.ds(2 * x, 2)], gf.at[x, chunk(c)], local_sem.at[CHUNKS + 2 + c]
        )
        for c in range(CHUNKS)
    ]
    out_fil = [
        pltpu.make_async_copy(
            fil.at[chunk(c)], filtered_out.at[chunk(c), 0], local_sem.at[2 * CHUNKS + 2 + c]
        )
        for c in range(CHUNKS)
    ]
    own_ritz = [
        pltpu.make_async_copy(
            sm.at[xp, x], ritz_out.at[:, 0, 2 * x + xp], local_sem.at[3 * CHUNKS + 2 + xp]
        )
        for xp in range(2)
    ]

    up0 = [
        remote(
            block.at[chunk(c), 0, :, pl.ds(2, 6), :],
            ext0.at[chunk(c), :, pl.ds(2, 6), :],
            halo_send.at[0, c],
            halo_recv.at[0, c],
            next_peer,
        )
        for c in range(CHUNKS)
    ]
    down0 = [
        remote(
            block.at[chunk(c), 0, :, pl.ds(0, 6), :],
            ext0.at[chunk(c), :, pl.ds(16, 6), :],
            halo_send.at[1, c],
            halo_recv.at[1, c],
            prev_peer,
        )
        for c in range(CHUNKS)
    ]
    up1 = [
        remote(
            ext1.at[chunk(c), :, pl.ds(10, 6), :],
            ext1.at[chunk(c), :, pl.ds(2, 6), :],
            halo_send.at[2, c],
            halo_recv.at[2, c],
            next_peer,
        )
        for c in range(CHUNKS)
    ]
    down1 = [
        remote(
            ext1.at[chunk(c), :, pl.ds(8, 6), :],
            ext1.at[chunk(c), :, pl.ds(16, 6), :],
            halo_send.at[3, c],
            halo_recv.at[3, c],
            prev_peer,
        )
        for c in range(CHUNKS)
    ]

    weights_x = [
        remote(prior_rot, wp.at[x], wp_send.at[r - 1], wp_recv.at[r - 1], x_peer(r)) for r in range(1, XS)
    ]
    prior_x = [
        [
            remote(
                prior.at[:, 0, 2 * x_of(r) + xp],
                gp.at[xp, x],
                gp_send.at[xp, r - 1],
                gp_recv.at[xp, r - 1],
                x_peer(r),
            )
            for r in range(1, XS)
        ]
        for xp in range(2)
    ]
    fil_x = [
        [
            remote(
                fil.at[chunk(c), pl.ds(2 * x_of(r), 2)],
                gf.at[x, chunk(c)],
                gf_send.at[c, r - 1],
                gf_recv.at[c, r - 1],
                x_peer(r),
            )
            for r in range(1, XS)
        ]
        for c in range(CHUNKS)
    ]

    def z_copy(xp, xd):
        rows = pl.ds((xd * ZH + (1 - zh)) * NB, NB)
        return remote(pp.at[xp, rows], zr.at[xp, xd], z_send.at[xp, xd], z_recv.at[xp, xd], z_peer)

    def out_copy(xp, r):
        return remote(
            sm.at[xp, x_of(r)],
            ritz_out.at[:, 0, 2 * x + xp],
            out_send.at[xp, r - 1],
            out_recv.at[xp, r - 1],
            x_peer(r),
        )

    for copy in own_block + own_prior:
        copy.start()

    row = lax.broadcasted_iota(jnp.int32, (CZ, CZ), 0)
    col = lax.broadcasted_iota(jnp.int32, (CZ, CZ), 1)
    apart = jnp.abs(row - col)
    taps = jnp.zeros((CZ, CZ), f32)
    for k in range(1, reach + 1):
        taps = jnp.where(apart == k, lap_scale * stencil_taps[k], taps)
    taps_high, taps_low = split(taps)
    band[0:CZ, :] = taps_high
    band[CZ : 2 * CZ, :] = taps_high
    band[2 * CZ : 3 * CZ, :] = taps_low
    diagonal[...] = pot[0] * (1.0 / half_range) + (
        3.0 * lap_scale * stencil_taps[0] - shift_center / half_range
    )

    @pl.when(jnp.logical_not(has_prev))
    def _():
        ext0[:, :, 0:8, :] = jnp.zeros((NB, CX, 8, CZ), f32)
        ext1[:, :, 0:8, :] = jnp.zeros((NB, CX, 8, CZ), f32)

    @pl.when(jnp.logical_not(has_next))
    def _():
        ext0[:, :, 16:24, :] = jnp.zeros((NB, CX, 8, CZ), f32)
        ext1[:, :, 16:24, :] = jnp.zeros((NB, CX, 8, CZ), f32)

    pl.semaphore_wait(
        barrier, XS + jnp.where(has_prev, 1, 0) + jnp.where(has_next, 1, 0)
    )

    def start_halo(up, down):
        @pl.when(has_next)
        def _():
            up.start()

        @pl.when(has_prev)
        def _():
            down.start()

    def wait_halo(up, down):
        @pl.when(has_prev)
        def _():
            up.wait_recv()

        @pl.when(has_next)
        def _():
            down.wait_recv()

    for c in range(CHUNKS):
        start_halo(up0[c], down0[c])
    for copy in weights_x + prior_x[0]:
        copy.start()

    for c in range(CHUNKS):
        own_block[c].wait()
        wait_halo(up0[c], down0[c])

        def first(j, carry):
            at = c * PER + j
            rows = stencil(ext0, at, band, diagonal)
            for i in range(CX):
                ext1[at, i, 8:16, :] = rows[i]
            return carry

        lax.fori_loop(0, PER, first, 0)
        start_halo(up1[c], down1[c])

    for c in range(CHUNKS):
        wait_halo(up1[c], down1[c])

        def second(j, carry):
            at = c * PER + j
            rows = stencil(ext1, at, band, diagonal)
            for i in range(CX):
                fil[at, i] = 2.0 * rows[i] - ext0[at, i, 8:16, :]
            return carry

        lax.fori_loop(0, PER, second, 0)
        for copy in fil_x[c] + [own_fil[c], out_fil[c]]:
            copy.start()
    for copy in prior_x[1]:
        copy.start()

    wp[x] = prior_rot[...]
    for copy in weights_x:
        copy.wait_recv()
    turned = jnp.concatenate([wp[s] for s in range(XS)], axis=0).T
    wp_high[...], wp_low[...] = split(turned)
    own_rows = jnp.concatenate(
        [block_rot[pl.ds(pl.multiple_of((s * ZH + zh) * NB, NB), NB), :] for s in range(XS)], axis=0
    )
    rows_high, rows_low = split(own_rows)
    stacked = jnp.concatenate([rows_high, rows_high, rows_low], axis=0).astype(f32)
    wf[...] = stacked.T.astype(bf16)

    gf_rows = gf.reshape(XS * NB * 2 * CY, CZ)

    def prior_part(xp):
        own_prior[xp].wait()
        for copy in prior_x[xp]:
            copy.wait_recv()
        gp_rows = gp.at[xp].reshape(XS * NP * CY, CZ)
        pp_rows = pp.at[xp].reshape(NCOL * CY, CZ)
        for y in range(0, CY, 2):
            values = jnp.concatenate(
                [gp_rows[pl.ds(y + h, XS * NP, stride=CY), :] for h in range(2)], axis=1
            )
            high, low = split(values)
            total = dot(wp_high[...], high) + dot(wp_high[...], low) + dot(wp_low[...], high)
            for h in range(2):
                pp_rows[pl.ds(y + h, NCOL, stride=CY), :] = total[:, h * CZ : (h + 1) * CZ]

    def block_part(xp):
        pp_rows = pp.at[xp].reshape(NCOL * CY, CZ)
        for y in range(0, CY, 2):
            values = jnp.concatenate(
                [gf_rows[pl.ds(xp * CY + y + h, XS * NB, stride=2 * CY), :] for h in range(2)], axis=1
            )
            high, low = split(values)
            total = dot(wf[...], jnp.concatenate([high, low, high], axis=0))
            for h in range(2):
                at = pl.ds(y + h, NCOL, stride=CY)
                pp_rows[at, :] = pp_rows[at, :] + total[:, h * CZ : (h + 1) * CZ]
        for xd in range(XS):
            z_copy(xp, xd).start()

    prior_part(0)
    for c in range(CHUNKS):
        own_fil[c].wait()
        for copy in fil_x[c]:
            copy.wait_recv()
    block_part(0)
    prior_part(1)
    block_part(1)

    for xp in range(2):
        for xd in range(XS):
            z_copy(xp, xd).wait_recv()
            sm[xp, xd] = pp[xp, pl.ds((xd * ZH + zh) * NB, NB)] + zr[xp, xd]
        for r in range(1, XS):
            out_copy(xp, r).start()
        own_ritz[xp].start()

    for xp in range(2):
        own_ritz[xp].wait()
        for r in range(1, XS):
            out_copy(xp, r).wait()
        for xd in range(XS):
            z_copy(xp, xd).wait_send()
        for copy in prior_x[xp]:
            copy.wait_send()
    for copy in weights_x:
        copy.wait_send()
    for c in range(CHUNKS):
        out_fil[c].wait()
        for copy in fil_x[c]:
            copy.wait_send()

        @pl.when(has_next)
        def _():
            up0[c].wait_send()
            up1[c].wait_send()

        @pl.when(has_prev)
        def _():
            down0[c].wait_send()
            down1[c].wait_send()


def shards(prior_orbitals, orbital_block, potential, prior_rotation, block_rotation):
    slabs = lax.axis_size("space")
    whole = pl.BlockSpec(memory_space=pltpu.VMEM)
    anywhere = pl.BlockSpec(memory_space=pl.ANY)
    dma = pltpu.SemaphoreType.DMA
    return pl.pallas_call(
        functools.partial(kernel, slabs),
        out_shape=(
            jax.ShapeDtypeStruct((NB, 1, CX, CY, CZ), f32),
            jax.ShapeDtypeStruct((NB, 1, CX, CY, CZ), f32),
        ),
        in_specs=[anywhere, anywhere, whole, whole, whole],
        out_specs=(anywhere, anywhere),
        scratch_shapes=[
            pltpu.VMEM((NB, CX, 24, CZ), f32),
            pltpu.VMEM((NB, CX, 24, CZ), f32),
            pltpu.VMEM((NB, CX, CY, CZ), f32),
            pltpu.VMEM((2, XS, NP, CY, CZ), f32),
            pltpu.VMEM((XS, NB, 2, CY, CZ), f32),
            pltpu.VMEM((XS, NP, NCOL), f32),
            pltpu.VMEM((NCOL, XS * NP), bf16),
            pltpu.VMEM((NCOL, XS * NP), bf16),
            pltpu.VMEM((NCOL, 3 * XS * NB), bf16),
            pltpu.VMEM((3 * CZ, CZ), bf16),
            pltpu.VMEM((CX, CY, CZ), f32),
            pltpu.VMEM((2, NCOL, CY, CZ), f32),
            pltpu.VMEM((2, XS, NB, CY, CZ), f32),
            pltpu.VMEM((2, XS, NB, CY, CZ), f32),
            dma((3 * CHUNKS + 4,)),
            dma((4, CHUNKS)),
            dma((4, CHUNKS)),
            dma((XS - 1,)),
            dma((XS - 1,)),
            dma((2, XS - 1)),
            dma((2, XS - 1)),
            dma((CHUNKS, XS - 1)),
            dma((CHUNKS, XS - 1)),
            dma((2, XS)),
            dma((2, XS)),
            dma((2, XS - 1)),
            dma((2, XS - 1)),
        ],
        compiler_params=pltpu.CompilerParams(
            collective_id=0, has_side_effects=True, vmem_limit_bytes=56 * 1024 * 1024
        ),
        cost_estimate=pl.CostEstimate(
            flops=3 * 2 * 256 * 128 * 2048, bytes_accessed=4 * 1024 * 1024, transcendentals=0
        ),
        name="filter_and_rotate",
    )(prior_orbitals, orbital_block, potential, prior_rotation, block_rotation)


def solution(mesh):
    placed = (
        P("band", "space", None, None, None),
        P("band", "space", None, None, None),
        P("space", None, None, None),
        P("band", None),
        P(),
    )
    return jax.shard_map(
        shards,
        mesh=mesh,
        in_specs=placed,
        out_specs=(P("band", "space", None, None, None), P("band", "space", None, None, None)),
        check_vma=False,
    )
```

```python
import functools

import jax
import jax.numpy as jnp
from jax import lax
from jax.experimental import pallas as pl
from jax.experimental.pallas import tpu as pltpu
from jax.sharding import PartitionSpec as P

stencil_taps = (
    -5369.0 / 1800.0,
    12.0 / 7.0,
    -15.0 / 56.0,
    10.0 / 189.0,
    -1.0 / 112.0,
    2.0 / 1925.0,
    -1.0 / 16632.0,
)
reach = 6
shift_center = 6.0
half_range = 5.0
lap_scale = -0.5 / half_range

NB = 16
NP = 48
CX = 8
CY = 8
CZ = 128
XS = 4
ZH = 2
NCOL = 128
CHUNKS = 4
WINDOW = 16
LAG = 8
HALF = CY // 2
ORDER = (2, 1, 3, 0)
PER = NB // CHUNKS
MESH = pl.DeviceIdType.MESH
f32 = jnp.float32
bf16 = jnp.bfloat16


def split(values):
    high = values.astype(bf16)
    low = (values - high.astype(f32)).astype(bf16)
    return high, low


def dot(lhs, rhs):
    return jnp.dot(lhs, rhs, preferred_element_type=f32)


def stencil(ext, at, band, diagonal):
    cells = ext[at, :, 8:16, :]
    high, low = split(cells.reshape(CX * CY, CZ))
    along_z = dot(jnp.concatenate([high, low, high], axis=1), band[...]).reshape(CX, CY, CZ)
    planes = [cells[i] for i in range(CX)]
    rows = []
    for i in range(CX):
        total = along_z[i] + diagonal[i] * planes[i]
        for k in range(1, reach + 1):
            near = ext[at, i, 8 - k : 16 - k, :] + ext[at, i, 8 + k : 16 + k, :]
            if i - k >= 0:
                near = near + planes[i - k]
            if i + k < CX:
                near = near + planes[i + k]
            total = total + (lap_scale * stencil_taps[k]) * near
        rows.append(total)
    return rows


def kernel(
    slabs,
    prior,
    block,
    pot,
    prior_rot,
    block_rot,
    fil,
    ritz_out,
    ext0,
    ext1,
    gp,
    gf,
    wp,
    wp_high,
    wp_low,
    wf,
    band,
    diagonal,
    pp,
    zr,
    sm,
    local_sem,
    halo_send,
    halo_recv,
    wp_send,
    wp_recv,
    gp_send,
    gp_recv,
    gf_send,
    gf_recv,
    z_send,
    z_recv,
    out_send,
    out_recv,
    z_ready,
):
    b = lax.axis_index("band")
    d = lax.axis_index("space")
    x = lax.div(b, ZH)
    zh = lax.rem(b, ZH)
    has_prev = d > 0
    has_next = d < slabs - 1

    def x_of(r):
        return lax.rem(x + r, XS)

    def x_peer(r):
        return (x_of(r) * ZH + zh, d)

    z_peer = (x * ZH + (1 - zh), d)
    prev_peer = (b, jnp.maximum(d - 1, 0))
    next_peer = (b, jnp.minimum(d + 1, slabs - 1))

    barrier = pltpu.get_barrier_semaphore()
    for r in range(1, XS):
        pl.semaphore_signal(barrier, inc=1, device_id=x_peer(r), device_id_type=MESH)

    @pl.when(zh == 0)
    def _():
        pl.semaphore_signal(barrier, inc=1, device_id=z_peer, device_id_type=MESH)

    @pl.when(has_prev)
    def _():
        pl.semaphore_signal(barrier, inc=1, device_id=prev_peer, device_id_type=MESH)

    @pl.when(has_next)
    def _():
        pl.semaphore_signal(barrier, inc=1, device_id=next_peer, device_id_type=MESH)

    def remote(src, dst, send, recv, peer):
        return pltpu.make_async_remote_copy(
            src_ref=src, dst_ref=dst, send_sem=send, recv_sem=recv, device_id=peer, device_id_type=MESH
        )

    parts = [(xp, yh, pl.ds(yh * HALF, HALF)) for xp in range(2) for yh in range(2)]

    def chunk(c):
        return pl.ds(c * PER, PER)

    own_block = [
        pltpu.make_async_copy(block.at[chunk(c), 0], ext0.at[chunk(c), :, pl.ds(8, 8), :], local_sem.at[c])
        for c in range(CHUNKS)
    ]
    own_prior = [
        pltpu.make_async_copy(
            prior.at[:, 0, 2 * x + xp, half], gp.at[xp, x, :, half], local_sem.at[2 * CHUNKS + 2 * xp + yh]
        )
        for xp, yh, half in parts
    ]
    own_fil = [
        pltpu.make_async_copy(
            fil.at[chunk(c), 0, pl.ds(2 * x, 2)], gf.at[x, chunk(c)], local_sem.at[CHUNKS + c]
        )
        for c in range(CHUNKS)
    ]

    up0 = [
        remote(
            block.at[chunk(c), 0, :, pl.ds(2, 6), :],
            ext0.at[chunk(c), :, pl.ds(2, 6), :],
            halo_send.at[0, c],
            halo_recv.at[0, c],
            next_peer,
        )
        for c in range(CHUNKS)
    ]
    down0 = [
        remote(
            block.at[chunk(c), 0, :, pl.ds(0, 6), :],
            ext0.at[chunk(c), :, pl.ds(16, 6), :],
            halo_send.at[1, c],
            halo_recv.at[1, c],
            prev_peer,
        )
        for c in range(CHUNKS)
    ]
    up1 = [
        remote(
            ext1.at[chunk(c), :, pl.ds(10, 6), :],
            ext1.at[chunk(c), :, pl.ds(2, 6), :],
            halo_send.at[2, c],
            halo_recv.at[2, c],
            next_peer,
        )
        for c in range(CHUNKS)
    ]
    down1 = [
        remote(
            ext1.at[chunk(c), :, pl.ds(8, 6), :],
            ext1.at[chunk(c), :, pl.ds(16, 6), :],
            halo_send.at[3, c],
            halo_recv.at[3, c],
            prev_peer,
        )
        for c in range(CHUNKS)
    ]

    weights_x = [
        remote(prior_rot, wp.at[x], wp_send.at[r - 1], wp_recv.at[r - 1], x_peer(r)) for r in range(1, XS)
    ]
    prior_x = [
        [
            remote(
                prior.at[:, 0, 2 * x_of(r) + xp, half],
                gp.at[xp, x, :, half],
                gp_send.at[2 * xp + yh, r - 1],
                gp_recv.at[2 * xp + yh, r - 1],
                x_peer(r),
            )
            for r in range(1, XS)
        ]
        for xp, yh, half in parts
    ]
    fil_x = [
        [
            remote(
                fil.at[chunk(c), 0, pl.ds(2 * x_of(r), 2)],
                gf.at[x, chunk(c)],
                gf_send.at[c, r - 1],
                gf_recv.at[c, r - 1],
                x_peer(r),
            )
            for r in range(1, XS)
        ]
        for c in range(CHUNKS)
    ]

    def z_copy(q, r):
        xp, _, half = parts[q]
        xd = x_of(r)
        rows = pl.ds((xd * ZH + (1 - zh)) * NB, NB)
        return remote(
            pp.at[xp, rows, half], zr.at[xp, xd, :, half], z_send.at[q, r], z_recv.at[q, r], z_peer
        )

    def out_copy(q, r):
        xp, _, half = parts[q]
        return remote(
            sm.at[xp, x_of(r), :, half],
            ritz_out.at[:, 0, 2 * x + xp, half],
            out_send.at[q, r - 1],
            out_recv.at[q, r - 1],
            x_peer(r),
        )

    for copy in own_block + own_prior:
        copy.start()

    row = lax.broadcasted_iota(jnp.int32, (CZ, CZ), 0)
    col = lax.broadcasted_iota(jnp.int32, (CZ, CZ), 1)
    apart = jnp.abs(row - col)
    taps = jnp.zeros((CZ, CZ), f32)
    for k in range(1, reach + 1):
        taps = jnp.where(apart == k, lap_scale * stencil_taps[k], taps)
    taps_high, taps_low = split(taps)
    band[0:CZ, :] = taps_high
    band[CZ : 2 * CZ, :] = taps_high
    band[2 * CZ : 3 * CZ, :] = taps_low
    diagonal[...] = pot[0] * (1.0 / half_range) + (
        3.0 * lap_scale * stencil_taps[0] - shift_center / half_range
    )

    @pl.when(jnp.logical_not(has_prev))
    def _():
        ext0[:, :, 0:8, :] = jnp.zeros((NB, CX, 8, CZ), f32)
        ext1[:, :, 0:8, :] = jnp.zeros((NB, CX, 8, CZ), f32)

    @pl.when(jnp.logical_not(has_next))
    def _():
        ext0[:, :, 16:24, :] = jnp.zeros((NB, CX, 8, CZ), f32)
        ext1[:, :, 16:24, :] = jnp.zeros((NB, CX, 8, CZ), f32)

    pl.semaphore_wait(
        barrier,
        XS - 1 + jnp.where(zh == 1, 1, 0) + jnp.where(has_prev, 1, 0) + jnp.where(has_next, 1, 0),
    )

    def start_halo(up, down):
        @pl.when(has_next)
        def _():
            up.start()

        @pl.when(has_prev)
        def _():
            down.start()

    def wait_halo(up, down):
        @pl.when(has_prev)
        def _():
            up.wait_recv()

        @pl.when(has_next)
        def _():
            down.wait_recv()

    for c in range(CHUNKS):
        start_halo(up0[c], down0[c])
    for copy in weights_x + prior_x[0]:
        copy.start()

    @pl.when(zh == 1)
    def _():
        pl.semaphore_signal(z_ready, inc=1, device_id=z_peer, device_id_type=MESH)

    for c in range(CHUNKS):
        own_block[c].wait()
        wait_halo(up0[c], down0[c])

        def first(j, carry):
            at = c * PER + j
            rows = stencil(ext0, at, band, diagonal)
            for i in range(CX):
                ext1[at, i, 8:16, :] = rows[i]
            return carry

        lax.fori_loop(0, PER, first, 0)
        start_halo(up1[c], down1[c])

    for c in range(CHUNKS):
        wait_halo(up1[c], down1[c])

        def second(j, carry):
            at = c * PER + j
            rows = stencil(ext1, at, band, diagonal)
            for i in range(CX):
                fil[at, 0, i] = 2.0 * rows[i] - ext0[at, i, 8:16, :]
            return carry

        lax.fori_loop(0, PER, second, 0)
        for copy in fil_x[c] + [own_fil[c]]:
            copy.start()
    for copy in prior_x[1] + prior_x[2]:
        copy.start()

    wp[x] = prior_rot[...]
    for copy in weights_x:
        copy.wait_recv()
    turned = jnp.concatenate([wp[s] for s in range(XS)], axis=0).T
    wp_high[...], wp_low[...] = split(turned)
    own_rows = jnp.concatenate(
        [block_rot[pl.ds(pl.multiple_of((s * ZH + zh) * NB, NB), NB), :] for s in range(XS)], axis=0
    )
    rows_high, rows_low = split(own_rows)
    stacked = jnp.concatenate([rows_high, rows_high, rows_low], axis=0).astype(f32)
    wf[...] = stacked.T.astype(bf16)

    gf_rows = gf.reshape(XS * NB * 2 * CY, CZ)

    def prior_part(q):
        xp, yh, _ = parts[q]
        own_prior[q].wait()
        for copy in prior_x[q]:
            copy.wait_recv()
        gp_rows = gp.at[xp].reshape(XS * NP * CY, CZ)
        pp_rows = pp.at[xp].reshape(NCOL * CY, CZ)
        for y in range(yh * HALF, yh * HALF + HALF, 2):
            values = jnp.concatenate(
                [gp_rows[pl.ds(y + h, XS * NP, stride=CY), :] for h in range(2)], axis=1
            )
            high, low = split(values)
            total = dot(wp_high[...], high) + dot(wp_high[...], low) + dot(wp_low[...], high)
            for h in range(2):
                pp_rows[pl.ds(y + h, NCOL, stride=CY), :] = total[:, h * CZ : (h + 1) * CZ]

    def block_part(q):
        xp, yh, _ = parts[q]
        pp_rows = pp.at[xp].reshape(NCOL * CY, CZ)
        for y in range(yh * HALF, yh * HALF + HALF, 2):
            values = jnp.concatenate(
                [gf_rows[pl.ds(xp * CY + y + h, XS * NB, stride=2 * CY), :] for h in range(2)], axis=1
            )
            high, low = split(values)
            total = dot(wf[...], jnp.concatenate([high, low, high], axis=0))
            for h in range(2):
                at = pl.ds(y + h, NCOL, stride=CY)
                pp_rows[at, :] = pp_rows[at, :] + total[:, h * CZ : (h + 1) * CZ]

    def finish(q, r):
        xp, yh, half = parts[q]
        xd = x_of(r)
        low, high = yh * HALF, yh * HALF + HALF
        z_copy(q, r).wait_recv()
        columns = pp[xp, pl.ds((xd * ZH + zh) * NB, NB), low:high] + zr[xp, xd, :, low:high]
        if r == 0:
            ritz_out[:, 0, 2 * x + xp, low:high] = columns
        else:
            sm[xp, xd, :, low:high] = columns
            out_copy(q, r).start()

    prior_part(0)
    for c in range(CHUNKS):
        own_fil[c].wait()
        for copy in fil_x[c]:
            copy.wait_recv()

    @pl.when(zh == 0)
    def _():
        pl.semaphore_wait(z_ready, 1)

    steps = [(q, r) for q in range(4) for r in ORDER]
    for k, (q, r) in enumerate(steps):
        if k % XS == 0:
            if q > 0:
                prior_part(q)
            block_part(q)
            if q == 1:
                for copy in prior_x[3]:
                    copy.start()
        if k >= WINDOW:
            z_copy(*steps[k - WINDOW]).wait_send()
        z_copy(q, r).start()
        if k >= LAG:
            finish(*steps[k - LAG])
    for k in range(len(steps) - LAG, len(steps)):
        finish(*steps[k])

    for k in range(len(steps) - WINDOW, len(steps)):
        z_copy(*steps[k]).wait_send()
    for q in range(4):
        for r in range(1, XS):
            out_copy(q, r).wait()
        for copy in prior_x[q]:
            copy.wait_send()
    for copy in weights_x:
        copy.wait_send()
    for c in range(CHUNKS):
        for copy in fil_x[c]:
            copy.wait_send()

        @pl.when(has_next)
        def _():
            up0[c].wait_send()
            up1[c].wait_send()

        @pl.when(has_prev)
        def _():
            down0[c].wait_send()
            down1[c].wait_send()


def shards(prior_orbitals, orbital_block, potential, prior_rotation, block_rotation):
    slabs = lax.axis_size("space")
    whole = pl.BlockSpec(memory_space=pltpu.VMEM)
    anywhere = pl.BlockSpec(memory_space=pl.ANY)
    dma = pltpu.SemaphoreType.DMA
    return pl.pallas_call(
        functools.partial(kernel, slabs),
        out_shape=(
            pltpu.VMEM((NB, 1, CX, CY, CZ), f32),
            pltpu.VMEM((NB, 1, CX, CY, CZ), f32),
        ),
        in_specs=[anywhere, anywhere, whole, whole, whole],
        out_specs=(whole, whole),
        scratch_shapes=[
            pltpu.VMEM((NB, CX, 24, CZ), f32),
            pltpu.VMEM((NB, CX, 24, CZ), f32),
            pltpu.VMEM((2, XS, NP, CY, CZ), f32),
            pltpu.VMEM((XS, NB, 2, CY, CZ), f32),
            pltpu.VMEM((XS, NP, NCOL), f32),
            pltpu.VMEM((NCOL, XS * NP), bf16),
            pltpu.VMEM((NCOL, XS * NP), bf16),
            pltpu.VMEM((NCOL, 3 * XS * NB), bf16),
            pltpu.VMEM((3 * CZ, CZ), bf16),
            pltpu.VMEM((CX, CY, CZ), f32),
            pltpu.VMEM((2, NCOL, CY, CZ), f32),
            pltpu.VMEM((2, XS, NB, CY, CZ), f32),
            pltpu.VMEM((2, XS, NB, CY, CZ), f32),
            dma((2 * CHUNKS + 4,)),
            dma((4, CHUNKS)),
            dma((4, CHUNKS)),
            dma((XS - 1,)),
            dma((XS - 1,)),
            dma((4, XS - 1)),
            dma((4, XS - 1)),
            dma((CHUNKS, XS - 1)),
            dma((CHUNKS, XS - 1)),
            dma((4, XS)),
            dma((4, XS)),
            dma((4, XS - 1)),
            dma((4, XS - 1)),
            pltpu.SemaphoreType.REGULAR,
        ],
        compiler_params=pltpu.CompilerParams(
            collective_id=0, has_side_effects=True, vmem_limit_bytes=56 * 1024 * 1024
        ),
        cost_estimate=pl.CostEstimate(
            flops=3 * 2 * 256 * 128 * 2048, bytes_accessed=4 * 1024 * 1024, transcendentals=0
        ),
        name="filter_and_rotate",
    )(prior_orbitals, orbital_block, potential, prior_rotation, block_rotation)


def solution(mesh):
    placed = (
        P("band", "space", None, None, None),
        P("band", "space", None, None, None),
        P("space", None, None, None),
        P("band", None),
        P(),
    )
    return jax.shard_map(
        shards,
        mesh=mesh,
        in_specs=placed,
        out_specs=(P("band", "space", None, None, None), P("band", "space", None, None, None)),
        check_vma=False,
    )
```

```python
import functools

import jax
import jax.numpy as jnp
from jax import lax
from jax.experimental import pallas as pl
from jax.experimental.pallas import tpu as pltpu
from jax.sharding import PartitionSpec as P

stencil_taps = (
    -5369.0 / 1800.0,
    12.0 / 7.0,
    -15.0 / 56.0,
    10.0 / 189.0,
    -1.0 / 112.0,
    2.0 / 1925.0,
    -1.0 / 16632.0,
)
reach = 6
shift_center = 6.0
half_range = 5.0
lap_scale = -0.5 / half_range

NB = 16
NP = 48
CX = 8
CY = 8
CZ = 128
XS = 4
ZH = 2
NCOL = 128
CHUNKS = 4
LAG = 8
HALF = CY // 2
ORDER = (2, 1, 3, 0)
PER = NB // CHUNKS
MESH = pl.DeviceIdType.MESH
f32 = jnp.float32
bf16 = jnp.bfloat16


def split(values):
    high = values.astype(bf16)
    low = (values - high.astype(f32)).astype(bf16)
    return high, low


def dot(lhs, rhs):
    return jnp.dot(lhs, rhs, preferred_element_type=f32)


def stencil(ext, at, band, diagonal):
    cells = ext[at, :, 8:16, :]
    high, low = split(cells.reshape(CX * CY, CZ))
    along_z = dot(jnp.concatenate([high, low, high], axis=1), band[...]).reshape(CX, CY, CZ)
    planes = [cells[i] for i in range(CX)]
    rows = []
    for i in range(CX):
        total = along_z[i] + diagonal[i] * planes[i]
        for k in range(1, reach + 1):
            near = ext[at, i, 8 - k : 16 - k, :] + ext[at, i, 8 + k : 16 + k, :]
            if i - k >= 0:
                near = near + planes[i - k]
            if i + k < CX:
                near = near + planes[i + k]
            total = total + (lap_scale * stencil_taps[k]) * near
        rows.append(total)
    return rows


def kernel(
    slabs,
    prior,
    block,
    pot,
    prior_rot,
    block_rot,
    fil,
    ritz_out,
    ext0,
    ext1,
    gp,
    gf,
    wp,
    wp_high,
    wp_low,
    wf,
    band,
    diagonal,
    pp,
    zr,
    sm,
    local_sem,
    halo_send,
    halo_recv,
    wp_send,
    wp_recv,
    gp_send,
    gp_recv,
    gf_send,
    gf_recv,
    z_send,
    z_recv,
    out_send,
    out_recv,
    z_ready,
):
    b = lax.axis_index("band")
    d = lax.axis_index("space")
    x = lax.div(b, ZH)
    zh = lax.rem(b, ZH)
    has_prev = d > 0
    has_next = d < slabs - 1

    def x_of(r):
        return lax.rem(x + r, XS)

    def x_peer(r):
        return (x_of(r) * ZH + zh, d)

    z_peer = (x * ZH + (1 - zh), d)
    prev_peer = (b, jnp.maximum(d - 1, 0))
    next_peer = (b, jnp.minimum(d + 1, slabs - 1))

    barrier = pltpu.get_barrier_semaphore()
    for r in range(1, XS):
        pl.semaphore_signal(barrier, inc=1, device_id=x_peer(r), device_id_type=MESH)

    @pl.when(zh == 0)
    def _():
        pl.semaphore_signal(barrier, inc=1, device_id=z_peer, device_id_type=MESH)

    @pl.when(has_prev)
    def _():
        pl.semaphore_signal(barrier, inc=1, device_id=prev_peer, device_id_type=MESH)

    @pl.when(has_next)
    def _():
        pl.semaphore_signal(barrier, inc=1, device_id=next_peer, device_id_type=MESH)

    def remote(src, dst, send, recv, peer):
        return pltpu.make_async_remote_copy(
            src_ref=src, dst_ref=dst, send_sem=send, recv_sem=recv, device_id=peer, device_id_type=MESH
        )

    parts = [(xp, yh, pl.ds(yh * HALF, HALF)) for xp in range(2) for yh in range(2)]

    def chunk(c):
        return pl.ds(c * PER, PER)

    own_block = [
        pltpu.make_async_copy(block.at[chunk(c), 0], ext0.at[chunk(c), :, pl.ds(8, 8), :], local_sem.at[c])
        for c in range(CHUNKS)
    ]
    own_prior = [
        pltpu.make_async_copy(
            prior.at[:, 0, 2 * x + xp, half], gp.at[xp, x, :, half], local_sem.at[2 * CHUNKS + 2 * xp + yh]
        )
        for xp, yh, half in parts
    ]
    own_fil = [
        pltpu.make_async_copy(
            fil.at[chunk(c), 0, pl.ds(2 * x, 2)], gf.at[x, chunk(c)], local_sem.at[CHUNKS + c]
        )
        for c in range(CHUNKS)
    ]

    up0 = [
        remote(
            block.at[chunk(c), 0, :, pl.ds(2, 6), :],
            ext0.at[chunk(c), :, pl.ds(2, 6), :],
            halo_send.at[0, c],
            halo_recv.at[0, c],
            next_peer,
        )
        for c in range(CHUNKS)
    ]
    down0 = [
        remote(
            block.at[chunk(c), 0, :, pl.ds(0, 6), :],
            ext0.at[chunk(c), :, pl.ds(16, 6), :],
            halo_send.at[1, c],
            halo_recv.at[1, c],
            prev_peer,
        )
        for c in range(CHUNKS)
    ]
    up1 = [
        remote(
            ext1.at[chunk(c), :, pl.ds(10, 6), :],
            ext1.at[chunk(c), :, pl.ds(2, 6), :],
            halo_send.at[2, c],
            halo_recv.at[2, c],
            next_peer,
        )
        for c in range(CHUNKS)
    ]
    down1 = [
        remote(
            ext1.at[chunk(c), :, pl.ds(8, 6), :],
            ext1.at[chunk(c), :, pl.ds(16, 6), :],
            halo_send.at[3, c],
            halo_recv.at[3, c],
            prev_peer,
        )
        for c in range(CHUNKS)
    ]

    weights_x = [
        remote(prior_rot, wp.at[x], wp_send.at[r - 1], wp_recv.at[r - 1], x_peer(r)) for r in range(1, XS)
    ]
    prior_x = [
        [
            remote(
                prior.at[:, 0, 2 * x_of(r) + xp, half],
                gp.at[xp, x, :, half],
                gp_send.at[2 * xp + yh, r - 1],
                gp_recv.at[2 * xp + yh, r - 1],
                x_peer(r),
            )
            for r in range(1, XS)
        ]
        for xp, yh, half in parts
    ]
    fil_x = [
        [
            remote(
                fil.at[chunk(c), 0, pl.ds(2 * x_of(r), 2)],
                gf.at[x, chunk(c)],
                gf_send.at[c, r - 1],
                gf_recv.at[c, r - 1],
                x_peer(r),
            )
            for r in range(1, XS)
        ]
        for c in range(CHUNKS)
    ]

    def z_copy(q, r):
        xp, _, half = parts[q]
        xd = x_of(r)
        rows = pl.ds((xd * ZH + (1 - zh)) * NB, NB)
        return remote(
            pp.at[xp, rows, half], zr.at[xp, xd, :, half], z_send.at[q, r], z_recv.at[q, r], z_peer
        )

    def out_copy(q, r):
        xp, _, half = parts[q]
        return remote(
            sm.at[xp, x_of(r), :, half],
            ritz_out.at[:, 0, 2 * x + xp, half],
            out_send.at[q, r - 1],
            out_recv.at[q, r - 1],
            x_peer(r),
        )

    for copy in own_block + own_prior:
        copy.start()

    row = lax.broadcasted_iota(jnp.int32, (CZ, CZ), 0)
    col = lax.broadcasted_iota(jnp.int32, (CZ, CZ), 1)
    apart = jnp.abs(row - col)
    taps = jnp.zeros((CZ, CZ), f32)
    for k in range(1, reach + 1):
        taps = jnp.where(apart == k, lap_scale * stencil_taps[k], taps)
    taps_high, taps_low = split(taps)
    band[0:CZ, :] = taps_high
    band[CZ : 2 * CZ, :] = taps_high
    band[2 * CZ : 3 * CZ, :] = taps_low
    diagonal[...] = pot[0] * (1.0 / half_range) + (
        3.0 * lap_scale * stencil_taps[0] - shift_center / half_range
    )

    @pl.when(jnp.logical_not(has_prev))
    def _():
        ext0[:, :, 0:8, :] = jnp.zeros((NB, CX, 8, CZ), f32)
        ext1[:, :, 0:8, :] = jnp.zeros((NB, CX, 8, CZ), f32)

    @pl.when(jnp.logical_not(has_next))
    def _():
        ext0[:, :, 16:24, :] = jnp.zeros((NB, CX, 8, CZ), f32)
        ext1[:, :, 16:24, :] = jnp.zeros((NB, CX, 8, CZ), f32)

    pl.semaphore_wait(
        barrier,
        XS - 1 + jnp.where(zh == 1, 1, 0) + jnp.where(has_prev, 1, 0) + jnp.where(has_next, 1, 0),
    )

    def start_halo(up, down):
        @pl.when(has_next)
        def _():
            up.start()

        @pl.when(has_prev)
        def _():
            down.start()

    def wait_halo(up, down):
        @pl.when(has_prev)
        def _():
            up.wait_recv()

        @pl.when(has_next)
        def _():
            down.wait_recv()

    for c in range(CHUNKS):
        start_halo(up0[c], down0[c])
    for copy in weights_x + prior_x[0]:
        copy.start()

    @pl.when(zh == 1)
    def _():
        pl.semaphore_signal(z_ready, inc=1, device_id=z_peer, device_id_type=MESH)

    for c in range(CHUNKS):
        own_block[c].wait()
        wait_halo(up0[c], down0[c])

        def first(j, carry):
            at = c * PER + j
            rows = stencil(ext0, at, band, diagonal)
            for i in range(CX):
                ext1[at, i, 8:16, :] = rows[i]
            return carry

        lax.fori_loop(0, PER, first, 0)
        start_halo(up1[c], down1[c])

    for c in range(CHUNKS):
        wait_halo(up1[c], down1[c])

        def second(j, carry):
            at = c * PER + j
            rows = stencil(ext1, at, band, diagonal)
            for i in range(CX):
                fil[at, 0, i] = 2.0 * rows[i] - ext0[at, i, 8:16, :]
            return carry

        lax.fori_loop(0, PER, second, 0)
        for copy in fil_x[c] + [own_fil[c]]:
            copy.start()
    for copy in prior_x[1] + prior_x[2]:
        copy.start()

    wp[x] = prior_rot[...]
    for copy in weights_x:
        copy.wait_recv()
    turned = jnp.concatenate([wp[s] for s in range(XS)], axis=0).T
    wp_high[...], wp_low[...] = split(turned)
    own_rows = jnp.concatenate(
        [block_rot[pl.ds(pl.multiple_of((s * ZH + zh) * NB, NB), NB), :] for s in range(XS)], axis=0
    )
    rows_high, rows_low = split(own_rows)
    stacked = jnp.concatenate([rows_high, rows_high, rows_low], axis=0).astype(f32)
    wf[...] = stacked.T.astype(bf16)

    gf_rows = gf.reshape(XS * NB * 2 * CY, CZ)

    def prior_part(q):
        xp, yh, _ = parts[q]
        own_prior[q].wait()
        for copy in prior_x[q]:
            copy.wait_recv()
        gp_rows = gp.at[xp].reshape(XS * NP * CY, CZ)
        pp_rows = pp.at[xp].reshape(NCOL * CY, CZ)
        for y in range(yh * HALF, yh * HALF + HALF, 2):
            values = jnp.concatenate(
                [gp_rows[pl.ds(y + h, XS * NP, stride=CY), :] for h in range(2)], axis=1
            )
            high, low = split(values)
            total = dot(wp_high[...], high) + dot(wp_high[...], low) + dot(wp_low[...], high)
            for h in range(2):
                pp_rows[pl.ds(y + h, NCOL, stride=CY), :] = total[:, h * CZ : (h + 1) * CZ]

    def block_part(q):
        xp, yh, _ = parts[q]
        pp_rows = pp.at[xp].reshape(NCOL * CY, CZ)
        for y in range(yh * HALF, yh * HALF + HALF, 2):
            values = jnp.concatenate(
                [gf_rows[pl.ds(xp * CY + y + h, XS * NB, stride=2 * CY), :] for h in range(2)], axis=1
            )
            high, low = split(values)
            total = dot(wf[...], jnp.concatenate([high, low, high], axis=0))
            for h in range(2):
                at = pl.ds(y + h, NCOL, stride=CY)
                pp_rows[at, :] = pp_rows[at, :] + total[:, h * CZ : (h + 1) * CZ]

    def finish(q, r):
        xp, yh, half = parts[q]
        xd = x_of(r)
        low, high = yh * HALF, yh * HALF + HALF
        z_copy(q, r).wait_recv()
        columns = pp[xp, pl.ds((xd * ZH + zh) * NB, NB), low:high] + zr[xp, xd, :, low:high]
        if r == 0:
            ritz_out[:, 0, 2 * x + xp, low:high] = columns
        else:
            sm[xp, xd, :, low:high] = columns
            out_copy(q, r).start()

    prior_part(0)
    for c in range(CHUNKS):
        own_fil[c].wait()
        for copy in fil_x[c]:
            copy.wait_recv()

    @pl.when(zh == 0)
    def _():
        pl.semaphore_wait(z_ready, 1)

    steps = [(q, r) for q in range(4) for r in ORDER if q < 2 or r != 0] + [(2, 0), (3, 0)]
    begins = {steps.index((q, ORDER[0])): q for q in range(4)}
    for k, (q, r) in enumerate(steps):
        if k in begins:
            if q > 0:
                prior_part(q)
            block_part(q)
            if q == 1:
                for copy in prior_x[3]:
                    copy.start()
        z_copy(q, r).start()
        if k >= LAG:
            finish(*steps[k - LAG])
    for k in range(len(steps) - LAG, len(steps)):
        finish(*steps[k])

    for q, r in steps:
        z_copy(q, r).wait_send()
    for q in range(4):
        for r in range(1, XS):
            out_copy(q, r).wait()
        for copy in prior_x[q]:
            copy.wait_send()
    for copy in weights_x:
        copy.wait_send()
    for c in range(CHUNKS):
        for copy in fil_x[c]:
            copy.wait_send()

        @pl.when(has_next)
        def _():
            up0[c].wait_send()
            up1[c].wait_send()

        @pl.when(has_prev)
        def _():
            down0[c].wait_send()
            down1[c].wait_send()


def write_out(filtered, ritz, filtered_out, ritz_out, sem):
    copies = [
        pltpu.make_async_copy(filtered, filtered_out, sem.at[0]),
        pltpu.make_async_copy(ritz, ritz_out, sem.at[1]),
    ]
    for copy in copies:
        copy.start()
    for copy in copies:
        copy.wait()


def shards(prior_orbitals, orbital_block, potential, prior_rotation, block_rotation):
    slabs = lax.axis_size("space")
    whole = pl.BlockSpec(memory_space=pltpu.VMEM)
    anywhere = pl.BlockSpec(memory_space=pl.ANY)
    dma = pltpu.SemaphoreType.DMA
    kept = pl.pallas_call(
        functools.partial(kernel, slabs),
        out_shape=(
            pltpu.VMEM((NB, 1, CX, CY, CZ), f32),
            pltpu.VMEM((NB, 1, CX, CY, CZ), f32),
        ),
        in_specs=[anywhere, anywhere, whole, whole, whole],
        out_specs=(whole, whole),
        scratch_shapes=[
            pltpu.VMEM((NB, CX, 24, CZ), f32),
            pltpu.VMEM((NB, CX, 24, CZ), f32),
            pltpu.VMEM((2, XS, NP, CY, CZ), f32),
            pltpu.VMEM((XS, NB, 2, CY, CZ), f32),
            pltpu.VMEM((XS, NP, NCOL), f32),
            pltpu.VMEM((NCOL, XS * NP), bf16),
            pltpu.VMEM((NCOL, XS * NP), bf16),
            pltpu.VMEM((NCOL, 3 * XS * NB), bf16),
            pltpu.VMEM((3 * CZ, CZ), bf16),
            pltpu.VMEM((CX, CY, CZ), f32),
            pltpu.VMEM((2, NCOL, CY, CZ), f32),
            pltpu.VMEM((2, XS, NB, CY, CZ), f32),
            pltpu.VMEM((2, XS, NB, CY, CZ), f32),
            dma((2 * CHUNKS + 4,)),
            dma((4, CHUNKS)),
            dma((4, CHUNKS)),
            dma((XS - 1,)),
            dma((XS - 1,)),
            dma((4, XS - 1)),
            dma((4, XS - 1)),
            dma((CHUNKS, XS - 1)),
            dma((CHUNKS, XS - 1)),
            dma((4, XS)),
            dma((4, XS)),
            dma((4, XS - 1)),
            dma((4, XS - 1)),
            pltpu.SemaphoreType.REGULAR,
        ],
        compiler_params=pltpu.CompilerParams(
            collective_id=0, has_side_effects=True, vmem_limit_bytes=56 * 1024 * 1024
        ),
        cost_estimate=pl.CostEstimate(
            flops=3 * 2 * 256 * 128 * 2048, bytes_accessed=4 * 1024 * 1024, transcendentals=0
        ),
        name="filter_and_rotate",
    )(prior_orbitals, orbital_block, potential, prior_rotation, block_rotation)
    return pl.pallas_call(
        write_out,
        out_shape=(
            jax.ShapeDtypeStruct((NB, 1, CX, CY, CZ), f32),
            jax.ShapeDtypeStruct((NB, 1, CX, CY, CZ), f32),
        ),
        in_specs=[whole, whole],
        out_specs=(anywhere, anywhere),
        scratch_shapes=[dma((2,))],
        cost_estimate=pl.CostEstimate(flops=0, bytes_accessed=2 * 1024 * 1024, transcendentals=0),
        name="write_out",
    )(*[pltpu.with_memory_space_constraint(k, pltpu.VMEM) for k in kept])


def solution(mesh):
    placed = (
        P("band", "space", None, None, None),
        P("band", "space", None, None, None),
        P("space", None, None, None),
        P("band", None),
        P(),
    )
    return jax.shard_map(
        shards,
        mesh=mesh,
        in_specs=placed,
        out_specs=(P("band", "space", None, None, None), P("band", "space", None, None, None)),
        check_vma=False,
    )
```

```python
import functools

import jax
import jax.numpy as jnp
from jax import lax
from jax.experimental import pallas as pl
from jax.experimental.pallas import tpu as pltpu
from jax.sharding import PartitionSpec as P

stencil_taps = (
    -5369.0 / 1800.0,
    12.0 / 7.0,
    -15.0 / 56.0,
    10.0 / 189.0,
    -1.0 / 112.0,
    2.0 / 1925.0,
    -1.0 / 16632.0,
)
reach = 6
shift_center = 6.0
half_range = 5.0
lap_scale = -0.5 / half_range

NB = 16
NP = 48
CX = 8
CY = 8
CZ = 128
XS = 4
ZH = 2
NCOL = 128
CHUNKS = 8
LAG = 6
HALF = CY // 2
ORDER = (2, 1, 3, 0)
PER = NB // CHUNKS
MESH = pl.DeviceIdType.MESH
f32 = jnp.float32
bf16 = jnp.bfloat16


def split(values):
    high = values.astype(bf16)
    low = (values - high.astype(f32)).astype(bf16)
    return high, low


def dot(lhs, rhs):
    return jnp.dot(lhs, rhs, preferred_element_type=f32)


def stencil(ext, at, band, diagonal):
    cells = ext[at, :, 8:16, :]
    high, low = split(cells.reshape(CX * CY, CZ))
    along_z = dot(jnp.concatenate([high, low, high], axis=1), band[...]).reshape(CX, CY, CZ)
    planes = [cells[i] for i in range(CX)]
    rows = []
    for i in range(CX):
        total = along_z[i] + diagonal[i] * planes[i]
        for k in range(1, reach + 1):
            near = ext[at, i, 8 - k : 16 - k, :] + ext[at, i, 8 + k : 16 + k, :]
            if i - k >= 0:
                near = near + planes[i - k]
            if i + k < CX:
                near = near + planes[i + k]
            total = total + (lap_scale * stencil_taps[k]) * near
        rows.append(total)
    return rows


def kernel(
    slabs,
    prior,
    block,
    pot,
    prior_rot,
    block_rot,
    fil,
    ritz_out,
    ext0,
    ext1,
    gp,
    gf,
    wp,
    wp_high,
    wp_low,
    wf,
    band,
    diagonal,
    pp,
    zr,
    sm,
    local_sem,
    halo_send,
    halo_recv,
    wp_send,
    wp_recv,
    gp_send,
    gp_recv,
    gf_send,
    gf_recv,
    z_send,
    z_recv,
    out_send,
    out_recv,
    z_ready,
    x_ready,
):
    b = lax.axis_index("band")
    d = lax.axis_index("space")
    x = lax.div(b, ZH)
    zh = lax.rem(b, ZH)
    has_prev = d > 0
    has_next = d < slabs - 1

    def x_of(r):
        return lax.rem(x + r, XS)

    def x_peer(r):
        return (x_of(r) * ZH + zh, d)

    z_peer = (x * ZH + (1 - zh), d)
    prev_peer = (b, jnp.maximum(d - 1, 0))
    next_peer = (b, jnp.minimum(d + 1, slabs - 1))

    barrier = pltpu.get_barrier_semaphore()

    for r in range(1, XS):

        @pl.when(x < x_of(r))
        def _():
            pl.semaphore_signal(barrier, inc=1, device_id=x_peer(r), device_id_type=MESH)

    @pl.when(zh == 0)
    def _():
        pl.semaphore_signal(barrier, inc=1, device_id=z_peer, device_id_type=MESH)

    @pl.when(has_prev)
    def _():
        pl.semaphore_signal(barrier, inc=1, device_id=prev_peer, device_id_type=MESH)

    @pl.when(has_next)
    def _():
        pl.semaphore_signal(barrier, inc=1, device_id=next_peer, device_id_type=MESH)

    def remote(src, dst, send, recv, peer):
        return pltpu.make_async_remote_copy(
            src_ref=src, dst_ref=dst, send_sem=send, recv_sem=recv, device_id=peer, device_id_type=MESH
        )

    parts = [(xp, yh, pl.ds(yh * HALF, HALF)) for xp in range(2) for yh in range(2)]

    def chunk(c):
        return pl.ds(c * PER, PER)

    own_block = [
        pltpu.make_async_copy(block.at[chunk(c), 0], ext0.at[chunk(c), :, pl.ds(8, 8), :], local_sem.at[c])
        for c in range(CHUNKS)
    ]
    own_prior = [
        pltpu.make_async_copy(
            prior.at[:, 0, 2 * x + xp, half], gp.at[xp, x, :, half], local_sem.at[2 * CHUNKS + 2 * xp + yh]
        )
        for xp, yh, half in parts
    ]
    own_fil = [
        pltpu.make_async_copy(
            fil.at[chunk(c), 0, pl.ds(2 * x, 2)], gf.at[x, chunk(c)], local_sem.at[CHUNKS + c]
        )
        for c in range(CHUNKS)
    ]

    up0 = [
        remote(
            block.at[chunk(c), 0, :, pl.ds(2, 6), :],
            ext0.at[chunk(c), :, pl.ds(2, 6), :],
            halo_send.at[0, c],
            halo_recv.at[0, c],
            next_peer,
        )
        for c in range(CHUNKS)
    ]
    down0 = [
        remote(
            block.at[chunk(c), 0, :, pl.ds(0, 6), :],
            ext0.at[chunk(c), :, pl.ds(16, 6), :],
            halo_send.at[1, c],
            halo_recv.at[1, c],
            prev_peer,
        )
        for c in range(CHUNKS)
    ]
    up1 = [
        remote(
            ext1.at[chunk(c), :, pl.ds(10, 6), :],
            ext1.at[chunk(c), :, pl.ds(2, 6), :],
            halo_send.at[2, c],
            halo_recv.at[2, c],
            next_peer,
        )
        for c in range(CHUNKS)
    ]
    down1 = [
        remote(
            ext1.at[chunk(c), :, pl.ds(8, 6), :],
            ext1.at[chunk(c), :, pl.ds(16, 6), :],
            halo_send.at[3, c],
            halo_recv.at[3, c],
            prev_peer,
        )
        for c in range(CHUNKS)
    ]

    weights_x = [
        remote(prior_rot, wp.at[x], wp_send.at[r - 1], wp_recv.at[r - 1], x_peer(r)) for r in range(1, XS)
    ]
    prior_x = [
        [
            remote(
                prior.at[:, 0, 2 * x_of(r) + xp, half],
                gp.at[xp, x, :, half],
                gp_send.at[2 * xp + yh, r - 1],
                gp_recv.at[2 * xp + yh, r - 1],
                x_peer(r),
            )
            for r in range(1, XS)
        ]
        for xp, yh, half in parts
    ]
    fil_x = [
        [
            remote(
                fil.at[chunk(c), 0, pl.ds(2 * x_of(r), 2)],
                gf.at[x, chunk(c)],
                gf_send.at[c, r - 1],
                gf_recv.at[c, r - 1],
                x_peer(r),
            )
            for r in range(1, XS)
        ]
        for c in range(CHUNKS)
    ]

    def z_copy(q, r):
        xp, _, half = parts[q]
        xd = x_of(r)
        rows = pl.ds((xd * ZH + (1 - zh)) * NB, NB)
        return remote(
            pp.at[xp, rows, half], zr.at[xp, xd, :, half], z_send.at[q, r], z_recv.at[q, r], z_peer
        )

    def out_copy(q, r):
        xp, _, half = parts[q]
        return remote(
            sm.at[xp, x_of(r), :, half],
            ritz_out.at[:, 0, 2 * x + xp, half],
            out_send.at[q, r - 1],
            out_recv.at[q, r - 1],
            x_peer(r),
        )

    for copy in own_block + own_prior:
        copy.start()

    row = lax.broadcasted_iota(jnp.int32, (CZ, CZ), 0)
    col = lax.broadcasted_iota(jnp.int32, (CZ, CZ), 1)
    apart = jnp.abs(row - col)
    taps = jnp.zeros((CZ, CZ), f32)
    for k in range(1, reach + 1):
        taps = jnp.where(apart == k, lap_scale * stencil_taps[k], taps)
    taps_high, taps_low = split(taps)
    band[0:CZ, :] = taps_high
    band[CZ : 2 * CZ, :] = taps_high
    band[2 * CZ : 3 * CZ, :] = taps_low
    diagonal[...] = pot[0] * (1.0 / half_range) + (
        3.0 * lap_scale * stencil_taps[0] - shift_center / half_range
    )

    @pl.when(jnp.logical_not(has_prev))
    def _():
        ext0[:, :, 0:8, :] = jnp.zeros((NB, CX, 8, CZ), f32)
        ext1[:, :, 0:8, :] = jnp.zeros((NB, CX, 8, CZ), f32)

    @pl.when(jnp.logical_not(has_next))
    def _():
        ext0[:, :, 16:24, :] = jnp.zeros((NB, CX, 8, CZ), f32)
        ext1[:, :, 16:24, :] = jnp.zeros((NB, CX, 8, CZ), f32)

    pl.semaphore_wait(
        barrier,
        x + jnp.where(zh == 1, 1, 0) + jnp.where(has_prev, 1, 0) + jnp.where(has_next, 1, 0),
    )

    def start_halo(up, down):
        @pl.when(has_next)
        def _():
            up.start()

        @pl.when(has_prev)
        def _():
            down.start()

    def wait_halo(up, down):
        @pl.when(has_prev)
        def _():
            up.wait_recv()

        @pl.when(has_next)
        def _():
            down.wait_recv()

    for c in range(CHUNKS):
        start_halo(up0[c], down0[c])
    for r in range(1, XS):

        @pl.when(x > x_of(r))
        def _():
            pl.semaphore_signal(x_ready, inc=1, device_id=x_peer(r), device_id_type=MESH)

    @pl.when(x < XS - 1)
    def _():
        pl.semaphore_wait(x_ready, XS - 1 - x)

    for copy in weights_x + prior_x[0]:
        copy.start()

    @pl.when(zh == 1)
    def _():
        pl.semaphore_signal(z_ready, inc=1, device_id=z_peer, device_id_type=MESH)

    for c in range(CHUNKS):
        own_block[c].wait()
        wait_halo(up0[c], down0[c])

        def first(j, carry):
            at = c * PER + j
            rows = stencil(ext0, at, band, diagonal)
            for i in range(CX):
                ext1[at, i, 8:16, :] = rows[i]
            return carry

        lax.fori_loop(0, PER, first, 0)
        start_halo(up1[c], down1[c])

    for c in range(CHUNKS):
        wait_halo(up1[c], down1[c])

        def second(j, carry):
            at = c * PER + j
            rows = stencil(ext1, at, band, diagonal)
            for i in range(CX):
                fil[at, 0, i] = 2.0 * rows[i] - ext0[at, i, 8:16, :]
            return carry

        lax.fori_loop(0, PER, second, 0)
        for copy in fil_x[c] + [own_fil[c]]:
            copy.start()
    for copy in prior_x[1] + prior_x[2]:
        copy.start()

    wp[x] = prior_rot[...]
    for copy in weights_x:
        copy.wait_recv()
    turned = jnp.concatenate([wp[s] for s in range(XS)], axis=0).T
    wp_high[...], wp_low[...] = split(turned)
    own_rows = jnp.concatenate(
        [block_rot[pl.ds(pl.multiple_of((s * ZH + zh) * NB, NB), NB), :] for s in range(XS)], axis=0
    )
    rows_high, rows_low = split(own_rows)
    stacked = jnp.concatenate([rows_high, rows_high, rows_low], axis=0).astype(f32)
    wf[...] = stacked.T.astype(bf16)

    gf_rows = gf.reshape(XS * NB * 2 * CY, CZ)

    def prior_part(q):
        xp, yh, _ = parts[q]
        own_prior[q].wait()
        for copy in prior_x[q]:
            copy.wait_recv()
        gp_rows = gp.at[xp].reshape(XS * NP * CY, CZ)
        pp_rows = pp.at[xp].reshape(NCOL * CY, CZ)
        for y in range(yh * HALF, yh * HALF + HALF, 2):
            values = jnp.concatenate(
                [gp_rows[pl.ds(y + h, XS * NP, stride=CY), :] for h in range(2)], axis=1
            )
            high, low = split(values)
            total = dot(wp_high[...], high) + dot(wp_high[...], low) + dot(wp_low[...], high)
            for h in range(2):
                pp_rows[pl.ds(y + h, NCOL, stride=CY), :] = total[:, h * CZ : (h + 1) * CZ]

    def block_part(q):
        xp, yh, _ = parts[q]
        pp_rows = pp.at[xp].reshape(NCOL * CY, CZ)
        for y in range(yh * HALF, yh * HALF + HALF, 2):
            values = jnp.concatenate(
                [gf_rows[pl.ds(xp * CY + y + h, XS * NB, stride=2 * CY), :] for h in range(2)], axis=1
            )
            high, low = split(values)
            total = dot(wf[...], jnp.concatenate([high, low, high], axis=0))
            for h in range(2):
                at = pl.ds(y + h, NCOL, stride=CY)
                pp_rows[at, :] = pp_rows[at, :] + total[:, h * CZ : (h + 1) * CZ]

    def finish(q, r):
        xp, yh, half = parts[q]
        xd = x_of(r)
        low, high = yh * HALF, yh * HALF + HALF
        z_copy(q, r).wait_recv()
        columns = pp[xp, pl.ds((xd * ZH + zh) * NB, NB), low:high] + zr[xp, xd, :, low:high]
        if r == 0:
            ritz_out[:, 0, 2 * x + xp, low:high] = columns
        else:
            sm[xp, xd, :, low:high] = columns
            out_copy(q, r).start()

    prior_part(0)
    for c in range(CHUNKS):
        own_fil[c].wait()
        for copy in fil_x[c]:
            copy.wait_recv()

    @pl.when(zh == 0)
    def _():
        pl.semaphore_wait(z_ready, 1)

    steps = [(q, r) for q in range(4) for r in ORDER if q < 2 or r != 0] + [(2, 0), (3, 0)]
    begins = {steps.index((q, ORDER[0])): q for q in range(4)}
    for k, (q, r) in enumerate(steps):
        if k in begins:
            if q > 0:
                prior_part(q)
            block_part(q)
            if q == 1:
                for copy in prior_x[3]:
                    copy.start()
        z_copy(q, r).start()
        if k >= LAG:
            finish(*steps[k - LAG])
    for k in range(len(steps) - LAG, len(steps)):
        finish(*steps[k])

    for q, r in steps:
        z_copy(q, r).wait_send()
    for q in range(4):
        for r in range(1, XS):
            out_copy(q, r).wait()
        for copy in prior_x[q]:
            copy.wait_send()
    for copy in weights_x:
        copy.wait_send()
    for c in range(CHUNKS):
        for copy in fil_x[c]:
            copy.wait_send()

        @pl.when(has_next)
        def _():
            up0[c].wait_send()
            up1[c].wait_send()

        @pl.when(has_prev)
        def _():
            down0[c].wait_send()
            down1[c].wait_send()


def write_out(filtered, ritz, filtered_out, ritz_out, sem):
    copies = [
        pltpu.make_async_copy(filtered, filtered_out, sem.at[0]),
        pltpu.make_async_copy(ritz, ritz_out, sem.at[1]),
    ]
    for copy in copies:
        copy.start()
    for copy in copies:
        copy.wait()


def shards(prior_orbitals, orbital_block, potential, prior_rotation, block_rotation):
    slabs = lax.axis_size("space")
    whole = pl.BlockSpec(memory_space=pltpu.VMEM)
    anywhere = pl.BlockSpec(memory_space=pl.ANY)
    dma = pltpu.SemaphoreType.DMA
    kept = pl.pallas_call(
        functools.partial(kernel, slabs),
        out_shape=(
            pltpu.VMEM((NB, 1, CX, CY, CZ), f32),
            pltpu.VMEM((NB, 1, CX, CY, CZ), f32),
        ),
        in_specs=[anywhere, anywhere, whole, whole, whole],
        out_specs=(whole, whole),
        scratch_shapes=[
            pltpu.VMEM((NB, CX, 24, CZ), f32),
            pltpu.VMEM((NB, CX, 24, CZ), f32),
            pltpu.VMEM((2, XS, NP, CY, CZ), f32),
            pltpu.VMEM((XS, NB, 2, CY, CZ), f32),
            pltpu.VMEM((XS, NP, NCOL), f32),
            pltpu.VMEM((NCOL, XS * NP), bf16),
            pltpu.VMEM((NCOL, XS * NP), bf16),
            pltpu.VMEM((NCOL, 3 * XS * NB), bf16),
            pltpu.VMEM((3 * CZ, CZ), bf16),
            pltpu.VMEM((CX, CY, CZ), f32),
            pltpu.VMEM((2, NCOL, CY, CZ), f32),
            pltpu.VMEM((2, XS, NB, CY, CZ), f32),
            pltpu.VMEM((2, XS, NB, CY, CZ), f32),
            dma((2 * CHUNKS + 4,)),
            dma((4, CHUNKS)),
            dma((4, CHUNKS)),
            dma((XS - 1,)),
            dma((XS - 1,)),
            dma((4, XS - 1)),
            dma((4, XS - 1)),
            dma((CHUNKS, XS - 1)),
            dma((CHUNKS, XS - 1)),
            dma((4, XS)),
            dma((4, XS)),
            dma((4, XS - 1)),
            dma((4, XS - 1)),
            pltpu.SemaphoreType.REGULAR,
            pltpu.SemaphoreType.REGULAR,
        ],
        compiler_params=pltpu.CompilerParams(
            collective_id=0, has_side_effects=True, vmem_limit_bytes=56 * 1024 * 1024
        ),
        cost_estimate=pl.CostEstimate(
            flops=3 * 2 * 256 * 128 * 2048, bytes_accessed=4 * 1024 * 1024, transcendentals=0
        ),
        name="filter_and_rotate",
    )(prior_orbitals, orbital_block, potential, prior_rotation, block_rotation)
    return pl.pallas_call(
        write_out,
        out_shape=(
            jax.ShapeDtypeStruct((NB, 1, CX, CY, CZ), f32),
            jax.ShapeDtypeStruct((NB, 1, CX, CY, CZ), f32),
        ),
        in_specs=[whole, whole],
        out_specs=(anywhere, anywhere),
        scratch_shapes=[dma((2,))],
        cost_estimate=pl.CostEstimate(flops=0, bytes_accessed=2 * 1024 * 1024, transcendentals=0),
        name="write_out",
    )(*[pltpu.with_memory_space_constraint(k, pltpu.VMEM) for k in kept])


def solution(mesh):
    placed = (
        P("band", "space", None, None, None),
        P("band", "space", None, None, None),
        P("space", None, None, None),
        P("band", None),
        P(),
    )
    return jax.shard_map(
        shards,
        mesh=mesh,
        in_specs=placed,
        out_specs=(P("band", "space", None, None, None), P("band", "space", None, None, None)),
        check_vma=False,
    )
```

```python
import functools

import jax
import jax.numpy as jnp
from jax import lax
from jax.experimental import pallas as pl
from jax.experimental.pallas import tpu as pltpu
from jax.sharding import PartitionSpec as P

stencil_taps = (
    -5369.0 / 1800.0,
    12.0 / 7.0,
    -15.0 / 56.0,
    10.0 / 189.0,
    -1.0 / 112.0,
    2.0 / 1925.0,
    -1.0 / 16632.0,
)
reach = 6
shift_center = 6.0
half_range = 5.0
lap_scale = -0.5 / half_range

NB = 16
NP = 48
CX = 8
CY = 8
CZ = 128
XS = 4
ZH = 2
NCOL = 128
CHUNKS = 8
LAG = 6
HALF = CY // 2
ORDER = (2, 1, 3, 0)
PER = NB // CHUNKS
MESH = pl.DeviceIdType.MESH
f32 = jnp.float32
bf16 = jnp.bfloat16


def split(values):
    high = values.astype(bf16)
    low = (values - high.astype(f32)).astype(bf16)
    return high, low


def dot(lhs, rhs):
    return jnp.dot(lhs, rhs, preferred_element_type=f32)


def stencil(ext, at, band, diagonal):
    cells = ext[at, :, 8:16, :]
    high, low = split(cells.reshape(CX * CY, CZ))
    along_z = dot(jnp.concatenate([high, low, high], axis=1), band[...]).reshape(CX, CY, CZ)
    planes = [cells[i] for i in range(CX)]
    rows = []
    for i in range(CX):
        total = along_z[i] + diagonal[i] * planes[i]
        for k in range(1, reach + 1):
            near = ext[at, i, 8 - k : 16 - k, :] + ext[at, i, 8 + k : 16 + k, :]
            if i - k >= 0:
                near = near + planes[i - k]
            if i + k < CX:
                near = near + planes[i + k]
            total = total + (lap_scale * stencil_taps[k]) * near
        rows.append(total)
    return rows


def kernel(
    slabs,
    prior,
    block,
    pot,
    prior_rot,
    block_rot,
    fil,
    ritz_out,
    ext0,
    ext1,
    gp,
    gf,
    wp,
    wp_high,
    wp_low,
    wf,
    band,
    diagonal,
    pp,
    zr,
    sm,
    local_sem,
    halo_send,
    halo_recv,
    wp_send,
    wp_recv,
    gp_send,
    gp_recv,
    gf_send,
    gf_recv,
    z_send,
    z_recv,
    out_send,
    out_recv,
    z_ready,
    x_ready,
):
    b = lax.axis_index("band")
    d = lax.axis_index("space")
    x = lax.div(b, ZH)
    zh = lax.rem(b, ZH)
    has_prev = d > 0
    has_next = d < slabs - 1

    def x_of(r):
        return lax.rem(x + r, XS)

    def x_peer(r):
        return (x_of(r) * ZH + zh, d)

    z_peer = (x * ZH + (1 - zh), d)
    prev_peer = (b, jnp.maximum(d - 1, 0))
    next_peer = (b, jnp.minimum(d + 1, slabs - 1))

    barrier = pltpu.get_barrier_semaphore()

    for r in range(1, XS):

        @pl.when(x < x_of(r))
        def _():
            pl.semaphore_signal(barrier, inc=1, device_id=x_peer(r), device_id_type=MESH)

    @pl.when(zh == 0)
    def _():
        pl.semaphore_signal(barrier, inc=1, device_id=z_peer, device_id_type=MESH)

    @pl.when(has_prev)
    def _():
        pl.semaphore_signal(barrier, inc=1, device_id=prev_peer, device_id_type=MESH)

    @pl.when(has_next)
    def _():
        pl.semaphore_signal(barrier, inc=1, device_id=next_peer, device_id_type=MESH)

    def remote(src, dst, send, recv, peer):
        return pltpu.make_async_remote_copy(
            src_ref=src, dst_ref=dst, send_sem=send, recv_sem=recv, device_id=peer, device_id_type=MESH
        )

    parts = [(xp, yh, pl.ds(yh * HALF, HALF)) for xp in range(2) for yh in range(2)]

    def chunk(c):
        return pl.ds(c * PER, PER)

    own_block = [
        pltpu.make_async_copy(block.at[chunk(c), 0], ext0.at[chunk(c), :, pl.ds(8, 8), :], local_sem.at[c])
        for c in range(CHUNKS)
    ]
    own_prior = [
        pltpu.make_async_copy(
            prior.at[:, 0, 2 * x + xp, half], gp.at[xp, x, :, half], local_sem.at[2 * CHUNKS + 2 * xp + yh]
        )
        for xp, yh, half in parts
    ]
    own_fil = [
        pltpu.make_async_copy(
            fil.at[chunk(c), 0, pl.ds(2 * x, 2)], gf.at[x, chunk(c)], local_sem.at[CHUNKS + c]
        )
        for c in range(CHUNKS)
    ]

    up0 = [
        remote(
            block.at[chunk(c), 0, :, pl.ds(2, 6), :],
            ext0.at[chunk(c), :, pl.ds(2, 6), :],
            halo_send.at[0, c],
            halo_recv.at[0, c],
            next_peer,
        )
        for c in range(CHUNKS)
    ]
    down0 = [
        remote(
            block.at[chunk(c), 0, :, pl.ds(0, 6), :],
            ext0.at[chunk(c), :, pl.ds(16, 6), :],
            halo_send.at[1, c],
            halo_recv.at[1, c],
            prev_peer,
        )
        for c in range(CHUNKS)
    ]
    up1 = [
        remote(
            ext1.at[chunk(c), :, pl.ds(10, 6), :],
            ext1.at[chunk(c), :, pl.ds(2, 6), :],
            halo_send.at[2, c],
            halo_recv.at[2, c],
            next_peer,
        )
        for c in range(CHUNKS)
    ]
    down1 = [
        remote(
            ext1.at[chunk(c), :, pl.ds(8, 6), :],
            ext1.at[chunk(c), :, pl.ds(16, 6), :],
            halo_send.at[3, c],
            halo_recv.at[3, c],
            prev_peer,
        )
        for c in range(CHUNKS)
    ]

    weights_x = [
        remote(prior_rot, wp.at[x], wp_send.at[r - 1], wp_recv.at[r - 1], x_peer(r)) for r in range(1, XS)
    ]
    prior_x = [
        [
            remote(
                prior.at[:, 0, 2 * x_of(r) + xp, half],
                gp.at[xp, x, :, half],
                gp_send.at[2 * xp + yh, r - 1],
                gp_recv.at[2 * xp + yh, r - 1],
                x_peer(r),
            )
            for r in range(1, XS)
        ]
        for xp, yh, half in parts
    ]
    fil_x = [
        [
            remote(
                fil.at[chunk(c), 0, pl.ds(2 * x_of(r), 2)],
                gf.at[x, chunk(c)],
                gf_send.at[c, r - 1],
                gf_recv.at[c, r - 1],
                x_peer(r),
            )
            for r in range(1, XS)
        ]
        for c in range(CHUNKS)
    ]

    def z_copy(q, r):
        xp, _, half = parts[q]
        xd = x_of(r)
        rows = pl.ds((xd * ZH + (1 - zh)) * NB, NB)
        return remote(
            pp.at[xp, rows, half], zr.at[xp, xd, :, half], z_send.at[q, r], z_recv.at[q, r], z_peer
        )

    def out_copy(q, r):
        xp, _, half = parts[q]
        return remote(
            sm.at[xp, x_of(r), :, half],
            ritz_out.at[:, 0, 2 * x + xp, half],
            out_send.at[q, r - 1],
            out_recv.at[q, r - 1],
            x_peer(r),
        )

    for copy in own_block + own_prior:
        copy.start()

    row = lax.broadcasted_iota(jnp.int32, (CZ, CZ), 0)
    col = lax.broadcasted_iota(jnp.int32, (CZ, CZ), 1)
    apart = jnp.abs(row - col)
    taps = jnp.zeros((CZ, CZ), f32)
    for k in range(1, reach + 1):
        taps = jnp.where(apart == k, lap_scale * stencil_taps[k], taps)
    taps_high, taps_low = split(taps)
    band[0:CZ, :] = taps_high
    band[CZ : 2 * CZ, :] = taps_high
    band[2 * CZ : 3 * CZ, :] = taps_low
    diagonal[...] = pot[0] * (1.0 / half_range) + (
        3.0 * lap_scale * stencil_taps[0] - shift_center / half_range
    )

    @pl.when(jnp.logical_not(has_prev))
    def _():
        ext0[:, :, 0:8, :] = jnp.zeros((NB, CX, 8, CZ), f32)
        ext1[:, :, 0:8, :] = jnp.zeros((NB, CX, 8, CZ), f32)

    @pl.when(jnp.logical_not(has_next))
    def _():
        ext0[:, :, 16:24, :] = jnp.zeros((NB, CX, 8, CZ), f32)
        ext1[:, :, 16:24, :] = jnp.zeros((NB, CX, 8, CZ), f32)

    pl.semaphore_wait(
        barrier,
        x + jnp.where(zh == 1, 1, 0) + jnp.where(has_prev, 1, 0) + jnp.where(has_next, 1, 0),
    )

    def start_halo(up, down):
        @pl.when(has_next)
        def _():
            up.start()

        @pl.when(has_prev)
        def _():
            down.start()

    def wait_halo(up, down):
        @pl.when(has_prev)
        def _():
            up.wait_recv()

        @pl.when(has_next)
        def _():
            down.wait_recv()

    for c in range(CHUNKS):
        start_halo(up0[c], down0[c])
    for r in range(1, XS):

        @pl.when(x > x_of(r))
        def _():
            pl.semaphore_signal(x_ready, inc=1, device_id=x_peer(r), device_id_type=MESH)

    @pl.when(x < XS - 1)
    def _():
        pl.semaphore_wait(x_ready, XS - 1 - x)

    for copy in weights_x + prior_x[0]:
        copy.start()

    @pl.when(zh == 1)
    def _():
        pl.semaphore_signal(z_ready, inc=1, device_id=z_peer, device_id_type=MESH)

    for c in range(CHUNKS):
        own_block[c].wait()
        wait_halo(up0[c], down0[c])

        def first(j, carry):
            at = c * PER + j
            rows = stencil(ext0, at, band, diagonal)
            for i in range(CX):
                ext1[at, i, 8:16, :] = rows[i]
            return carry

        lax.fori_loop(0, PER, first, 0)
        start_halo(up1[c], down1[c])

    for c in range(CHUNKS):
        wait_halo(up1[c], down1[c])

        def second(j, carry):
            at = c * PER + j
            rows = stencil(ext1, at, band, diagonal)
            for i in range(CX):
                fil[at, 0, i] = 2.0 * rows[i] - ext0[at, i, 8:16, :]
            return carry

        lax.fori_loop(0, PER, second, 0)
        for copy in (fil_x[c][1], fil_x[c][0], fil_x[c][2], own_fil[c]):
            copy.start()
    for copy in prior_x[1] + prior_x[2]:
        copy.start()

    wp[x] = prior_rot[...]
    for copy in weights_x:
        copy.wait_recv()
    turned = jnp.concatenate([wp[s] for s in range(XS)], axis=0).T
    wp_high[...], wp_low[...] = split(turned)
    own_rows = jnp.concatenate(
        [block_rot[pl.ds(pl.multiple_of((s * ZH + zh) * NB, NB), NB), :] for s in range(XS)], axis=0
    )
    rows_high, rows_low = split(own_rows)
    stacked = jnp.concatenate([rows_high, rows_high, rows_low], axis=0).astype(f32)
    wf[...] = stacked.T.astype(bf16)

    gf_rows = gf.reshape(XS * NB * 2 * CY, CZ)

    def prior_part(q):
        xp, yh, _ = parts[q]
        own_prior[q].wait()
        for copy in prior_x[q]:
            copy.wait_recv()
        gp_rows = gp.at[xp].reshape(XS * NP * CY, CZ)
        pp_rows = pp.at[xp].reshape(NCOL * CY, CZ)
        for y in range(yh * HALF, yh * HALF + HALF, 2):
            values = jnp.concatenate(
                [gp_rows[pl.ds(y + h, XS * NP, stride=CY), :] for h in range(2)], axis=1
            )
            high, low = split(values)
            total = dot(wp_high[...], high) + dot(wp_high[...], low) + dot(wp_low[...], high)
            for h in range(2):
                pp_rows[pl.ds(y + h, NCOL, stride=CY), :] = total[:, h * CZ : (h + 1) * CZ]

    def block_part(q):
        xp, yh, _ = parts[q]
        pp_rows = pp.at[xp].reshape(NCOL * CY, CZ)
        for y in range(yh * HALF, yh * HALF + HALF, 2):
            values = jnp.concatenate(
                [gf_rows[pl.ds(xp * CY + y + h, XS * NB, stride=2 * CY), :] for h in range(2)], axis=1
            )
            high, low = split(values)
            total = dot(wf[...], jnp.concatenate([high, low, high], axis=0))
            for h in range(2):
                at = pl.ds(y + h, NCOL, stride=CY)
                pp_rows[at, :] = pp_rows[at, :] + total[:, h * CZ : (h + 1) * CZ]

    def finish(q, r):
        xp, yh, half = parts[q]
        xd = x_of(r)
        low, high = yh * HALF, yh * HALF + HALF
        z_copy(q, r).wait_recv()
        columns = pp[xp, pl.ds((xd * ZH + zh) * NB, NB), low:high] + zr[xp, xd, :, low:high]
        if r == 0:
            ritz_out[:, 0, 2 * x + xp, low:high] = columns
        else:
            sm[xp, xd, :, low:high] = columns
            out_copy(q, r).start()

    prior_part(0)
    for c in range(CHUNKS):
        own_fil[c].wait()
        for copy in fil_x[c]:
            copy.wait_recv()

    @pl.when(zh == 0)
    def _():
        pl.semaphore_wait(z_ready, 1)

    steps = [(q, r) for q in range(4) for r in ORDER if q < 2 or r != 0] + [(2, 0), (3, 0)]
    begins = {steps.index((q, ORDER[0])): q for q in range(4)}
    for k, (q, r) in enumerate(steps):
        if k in begins:
            if q > 0:
                prior_part(q)
            block_part(q)
            if q == 1:
                for copy in prior_x[3]:
                    copy.start()
        z_copy(q, r).start()
        if k >= LAG:
            finish(*steps[k - LAG])
    for k in range(len(steps) - LAG, len(steps)):
        finish(*steps[k])

    for q, r in steps:
        z_copy(q, r).wait_send()
    for q in range(4):
        for r in range(1, XS):
            out_copy(q, r).wait()
        for copy in prior_x[q]:
            copy.wait_send()
    for copy in weights_x:
        copy.wait_send()
    for c in range(CHUNKS):
        for copy in fil_x[c]:
            copy.wait_send()

        @pl.when(has_next)
        def _():
            up0[c].wait_send()
            up1[c].wait_send()

        @pl.when(has_prev)
        def _():
            down0[c].wait_send()
            down1[c].wait_send()


def write_out(filtered, ritz, filtered_out, ritz_out, sem):
    copies = [
        pltpu.make_async_copy(filtered, filtered_out, sem.at[0]),
        pltpu.make_async_copy(ritz, ritz_out, sem.at[1]),
    ]
    for copy in copies:
        copy.start()
    for copy in copies:
        copy.wait()


def shards(prior_orbitals, orbital_block, potential, prior_rotation, block_rotation):
    slabs = lax.axis_size("space")
    whole = pl.BlockSpec(memory_space=pltpu.VMEM)
    anywhere = pl.BlockSpec(memory_space=pl.ANY)
    dma = pltpu.SemaphoreType.DMA
    kept = pl.pallas_call(
        functools.partial(kernel, slabs),
        out_shape=(
            pltpu.VMEM((NB, 1, CX, CY, CZ), f32),
            pltpu.VMEM((NB, 1, CX, CY, CZ), f32),
        ),
        in_specs=[anywhere, anywhere, whole, whole, whole],
        out_specs=(whole, whole),
        scratch_shapes=[
            pltpu.VMEM((NB, CX, 24, CZ), f32),
            pltpu.VMEM((NB, CX, 24, CZ), f32),
            pltpu.VMEM((2, XS, NP, CY, CZ), f32),
            pltpu.VMEM((XS, NB, 2, CY, CZ), f32),
            pltpu.VMEM((XS, NP, NCOL), f32),
            pltpu.VMEM((NCOL, XS * NP), bf16),
            pltpu.VMEM((NCOL, XS * NP), bf16),
            pltpu.VMEM((NCOL, 3 * XS * NB), bf16),
            pltpu.VMEM((3 * CZ, CZ), bf16),
            pltpu.VMEM((CX, CY, CZ), f32),
            pltpu.VMEM((2, NCOL, CY, CZ), f32),
            pltpu.VMEM((2, XS, NB, CY, CZ), f32),
            pltpu.VMEM((2, XS, NB, CY, CZ), f32),
            dma((2 * CHUNKS + 4,)),
            dma((4, CHUNKS)),
            dma((4, CHUNKS)),
            dma((XS - 1,)),
            dma((XS - 1,)),
            dma((4, XS - 1)),
            dma((4, XS - 1)),
            dma((CHUNKS, XS - 1)),
            dma((CHUNKS, XS - 1)),
            dma((4, XS)),
            dma((4, XS)),
            dma((4, XS - 1)),
            dma((4, XS - 1)),
            pltpu.SemaphoreType.REGULAR,
            pltpu.SemaphoreType.REGULAR,
        ],
        compiler_params=pltpu.CompilerParams(
            collective_id=0, has_side_effects=True, vmem_limit_bytes=56 * 1024 * 1024
        ),
        cost_estimate=pl.CostEstimate(
            flops=3 * 2 * 256 * 128 * 2048, bytes_accessed=4 * 1024 * 1024, transcendentals=0
        ),
        name="filter_and_rotate",
    )(prior_orbitals, orbital_block, potential, prior_rotation, block_rotation)
    return pl.pallas_call(
        write_out,
        out_shape=(
            jax.ShapeDtypeStruct((NB, 1, CX, CY, CZ), f32),
            jax.ShapeDtypeStruct((NB, 1, CX, CY, CZ), f32),
        ),
        in_specs=[whole, whole],
        out_specs=(anywhere, anywhere),
        scratch_shapes=[dma((2,))],
        cost_estimate=pl.CostEstimate(flops=0, bytes_accessed=2 * 1024 * 1024, transcendentals=0),
        name="write_out",
    )(*[pltpu.with_memory_space_constraint(k, pltpu.VMEM) for k in kept])


def solution(mesh):
    placed = (
        P("band", "space", None, None, None),
        P("band", "space", None, None, None),
        P("space", None, None, None),
        P("band", None),
        P(),
    )
    return jax.shard_map(
        shards,
        mesh=mesh,
        in_specs=placed,
        out_specs=(P("band", "space", None, None, None), P("band", "space", None, None, None)),
        check_vma=False,
    )
```
